32 devices in a mesh: tm: 4 (over x, core), space: 8 (over z, y).
Axes of the slice: x: 2, y: 2, z: 4, core: 2. Of those that a mesh axis runs over, the one named last changes fastest.
Arguments:
- starts: float32 [4, 32, 256, 384], P('tm', 'space'), may hold values from -18 to 18, as said below
- material: int32 [32, 256, 384], P('space'), may hold values from 0 to 7
- conductivity: float32 [8], replicated, may hold values from 0.3 to 3, as said below
Outputs:
- new_starts: float32 [4, 32, 256, 384], P('tm', 'space')
- coarse_path: float32 [4, 8, 64, 96], P('tm')
The draws below stay inside these ranges and needn't reach their ends.
Inputs may be any that keep to these rules, and one draw needn't show every extreme that they name: `starts`: start states of order one. `conductivity`: positive conductivities.
All inputs are finite; a program needn't handle non-finite values.
Results may differ from the reference program's by a relative error of at most 0.0001.
Values sent between devices are 32-bit elements; how exact they have to be, the bound alone decides.
A program may use at most 128 MiB of HBM per device.

```python
import math
import jax
import jax.numpy as jnp
from jax import lax

NY = 256
NZ = 384
FACTOR = 4
SUBSTEPS = 2
SWEEPS = 2
JACOBI = 3
REGIONS = 8
SLICES = 4
NX = 32


def draw_starts(key, part):
    key_base = jax.random.fold_in(jax.random.fold_in(key, 11), 0)
    position = (jnp.arange(NX, dtype=jnp.float32) + 0.5) / NX
    ramp = jnp.exp(math.log(3.0) * position)[None, :, None, None]
    base = jax.random.truncated_normal(key_base, -6.0, 6.0, (SLICES, NX, NY, NZ), jnp.float32)
    values = base * ramp
    return values.astype(jnp.float32)


def draw_material(key, part):
    key_pick, key_other = jax.random.split(jax.random.fold_in(key, 23))
    band = jnp.arange(NX, dtype=jnp.int32) * REGIONS // NX
    keep = jax.random.randint(key_pick, (NX, NY, NZ), 0, 4) < 3
    other = jax.random.randint(key_other, (NX, NY, NZ), 0, REGIONS)
    return jnp.where(keep, band[:, None, None], other).astype(jnp.int32)


def draw_conductivity(key, part):
    key_level = jax.random.fold_in(key, 37)
    level = jax.random.uniform(key_level, (REGIONS,), jnp.float32, 0.0, 1.0)
    ranks = jnp.arange(REGIONS, dtype=jnp.float32)
    exponent = (ranks + 1.5 * level) / (REGIONS + 0.5)
    values = 0.3 * jnp.exp(math.log(10.0) * exponent)
    return values.astype(jnp.float32)


def setup_inputs(seed: int = 0) -> dict:
    splits = jax.random.split(jax.random.key(seed), 4)
    return {
        "starts": draw_starts(jax.random.fold_in(splits[3], 71), 0),
        "material": draw_material(jax.random.fold_in(splits[3], 71), 0),
        "conductivity": draw_conductivity(jax.random.fold_in(splits[3], 71), 0),
    }


fine_step = 0.15
coarse_rate = 0.3
face_offsets = ((0, 1, 1), (2, 1, 1), (1, 0, 1), (1, 2, 1), (1, 1, 0), (1, 1, 2))

def window(padded, offsets, cells):
    return padded[offsets[0]:offsets[0] + cells[0], offsets[1]:offsets[1] + cells[1], offsets[2]:offsets[2] + cells[2]]

def laplace_apply(padded, cells):
    summed = jnp.zeros(cells, jnp.float32)
    for shift_x in range(3):
        for shift_y in range(3):
            for shift_z in range(3):
                moved_axes = int(shift_x != 1) + int(shift_y != 1) + int(shift_z != 1)
                if moved_axes == 0:
                    continue
                weight = 0.5 ** (moved_axes - 1)
                summed = summed + weight * window(padded, (shift_x, shift_y, shift_z), cells)
    return 14.0 * window(padded, (1, 1, 1), cells) - summed

def operate(vector, root_cond):
    scaled = root_cond * vector
    padded = jnp.pad(scaled, 1)
    return vector + fine_step * root_cond * laplace_apply(padded, vector.shape)

def substep(rhs_field, root_cond):
    iterate = rhs_field
    resid = rhs_field - operate(iterate, root_cond)
    direction = resid
    norm_now = jnp.sum(resid * resid)
    for sweep_index in range(SWEEPS):
        image = operate(direction, root_cond)
        step_len = norm_now / jnp.sum(direction * image)
        iterate = iterate + step_len * direction
        resid = resid - step_len * image
        if sweep_index + 1 < SWEEPS:
            norm_next = jnp.sum(resid * resid)
            direction = resid + norm_next / norm_now * direction
            norm_now = norm_next
    return iterate

def propagate(start_field, root_cond):
    current = start_field
    for step_index in range(SUBSTEPS):
        current = substep(current, root_cond)
    return current

def restrict(fine_field):
    size_x, size_y, size_z = fine_field.shape
    blocks = fine_field.reshape(size_x // FACTOR, FACTOR, size_y // FACTOR, FACTOR, size_z // FACTOR, FACTOR)
    return lax.optimization_barrier(jnp.mean(blocks, axis=(1, 3, 5)))

def prolong(coarse_field):
    size_x, size_y, size_z = coarse_field.shape
    spread = jnp.broadcast_to(coarse_field[:, None, :, None, :, None], (size_x, FACTOR, size_y, FACTOR, size_z, FACTOR))
    return spread.reshape(size_x * FACTOR, size_y * FACTOR, size_z * FACTOR)

def coarse_setup(coarse_k):
    padded_k = jnp.pad(coarse_k, 1, mode='edge')
    face_coefs = []
    diagonal = jnp.ones(coarse_k.shape, jnp.float32)
    for offsets in face_offsets:
        coef = coarse_rate * 0.5 * (coarse_k + window(padded_k, offsets, coarse_k.shape))
        face_coefs.append(coef)
        diagonal = diagonal + coef
    return (face_coefs, diagonal)

def coarse_step(source, face_coefs, diagonal):
    iterate = source
    for sweep_index in range(JACOBI):
        padded = jnp.pad(iterate, 1)
        summed = jnp.zeros(source.shape, jnp.float32)
        for coef, offsets in zip(face_coefs, face_offsets):
            summed = summed + coef * window(padded, offsets, source.shape)
        iterate = (source + summed) / diagonal
    return iterate

def reference(starts, material, conductivity):
    conduct = conductivity[material]
    root_cond = jnp.sqrt(conduct)

    def fine_one(start_field):
        return propagate(start_field, root_cond)
    fine_ends = lax.map(fine_one, starts)
    face_coefs, diagonal = coarse_setup(restrict(conduct))

    def coarse_one(start_field):
        return coarse_step(restrict(start_field), face_coefs, diagonal)
    coarse_old = lax.map(coarse_one, starts)
    coarse_ends = lax.map(restrict, fine_ends)
    jump_terms = coarse_ends - coarse_old

    def advance(carry_in, jump_term):
        stepped = coarse_step(carry_in, face_coefs, diagonal) + jump_term
        return (stepped, stepped)
    last_state, coarse_path = lax.scan(advance, restrict(starts[0]), jump_terms)
    corrections = jax.vmap(prolong)(coarse_path - coarse_ends)
    new_starts = jnp.concatenate([starts[:1], fine_ends[:-1] + corrections[:-1]], axis=0)
    return (new_starts, coarse_path)
```

```python
import functools

import jax
import jax.numpy as jnp
from jax import lax
from jax.experimental import pallas as pl
from jax.experimental.pallas import tpu as pltpu
from jax.sharding import PartitionSpec as P

FACTOR = 4
JACOBI = 3
W = 5
RH = 8
LANES = 128
HIGH = lax.Precision.HIGHEST
MESH = pl.DeviceIdType.MESH


def quarter(shape, long_axis):
    fine = lax.shift_right_logical(lax.broadcasted_iota(jnp.int32, shape, long_axis), 2)
    coarse = lax.broadcasted_iota(jnp.int32, shape, 1 - long_axis)
    return jnp.where(fine == coarse, 1.0, 0.0).astype(jnp.float32)


def mm(a, b):
    return jnp.dot(a, b, precision=HIGH, preferred_element_type=jnp.float32)


def kernel(
    T, S, L, NY, NZ, regions,
    cond_ref, st_ref, mat_ref,
    out_ref, path_ref,
    k_slab, b, k, ua, ub, r, q, xf, fe,
    red, gath, ce, pin, din, dsend, coefs, rdiag,
    b_recv, k_recv, b_ysend, k_ysend, b_zsend, k_zsend, k_sib,
    a_send, a_recv, g_send, g_recv, c_send, c_recv, e_send, e_recv, p_send, p_recv,
):
    tm = lax.axis_index("tm")
    s = lax.axis_index("space")
    h = lax.rem(s, 2)
    p = s // 2
    NP = S // 2
    PL = 2 * L
    E = PL + 2 * W
    HY = NY // 2
    RW = HY + RH
    RE = HY + 2 * RH
    partner = s + 1 - 2 * h
    par = lax.rem(tm, 2)
    sib = tm + 1 - 2 * par
    has_up = p < NP - 1
    has_dn = p > 0
    LC = L // FACTOR
    XC = LC * S
    YC = NY // FACTOR
    ZC = NZ // FACTOR

    def dev(t_, s_):
        return (t_, s_)

    def remote(src, dst, ss, rs, d):
        return pltpu.make_async_remote_copy(
            src_ref=src, dst_ref=dst, send_sem=ss, recv_sem=rs, device_id=d, device_id_type=MESH
        )

    own_off = pl.multiple_of(RH - RH * h, 8)
    own_src = pl.multiple_of((HY - RH) * h, 8)
    oth_off = pl.multiple_of(RH * h, 8)
    oth_src = pl.multiple_of((HY - RH) * (1 - h), 8)
    own_rows = pl.ds(own_off, RW)
    zero_rows = pl.ds(pl.multiple_of(h * RW, 8), RH)

    bar = pltpu.get_barrier_semaphore()
    for i in range(1, S):
        pl.semaphore_signal(bar, 1, device_id=dev(tm, lax.rem(s + i, S)), device_id_type=MESH)

    @pl.when(tm < T - 1)
    def _():
        pl.semaphore_signal(bar, 1, device_id=dev(tm + 1, s), device_id_type=MESH)
        pl.semaphore_signal(bar, 1, device_id=dev(tm + 1, partner), device_id_type=MESH)

    @pl.when(tm > 0)
    def _():
        pl.semaphore_signal(bar, 1, device_id=dev(tm - 1, s), device_id_type=MESH)
        pl.semaphore_signal(bar, 1, device_id=dev(tm - 1, partner), device_id_type=MESH)

    tm_peers = 2 * jnp.where(tm < T - 1, 1, 0) + 2 * jnp.where(tm > 0, 1, 0)
    pl.semaphore_wait(bar, S - 1 + tm_peers)

    def y_copy(slab, ext, t, ss, rs):
        e = W + h * L + t
        return remote(
            slab.at[t, pl.ds(oth_src, RW), :], ext.at[e, pl.ds(oth_off, RW), :],
            ss.at[t], rs.at[e], dev(tm, partner),
        )

    def plane_recv(ext, e, ss, rs):
        ref = ext.at[e, own_rows, :]
        return remote(ref, ref, ss, rs.at[e], dev(tm, partner))

    def z_copy(ext, pp, up, ss, rs):
        src = ext.at[W + pp, own_rows, :]
        if up:
            e = pp - PL + W
            return remote(src, ext.at[e, own_rows, :], ss.at[0, pp], rs.at[e], dev(tm, s + 2))
        e = pp + PL + W
        return remote(src, ext.at[e, own_rows, :], ss.at[1, pp], rs.at[e], dev(tm, s - 2))

    def z_each(ext, pp, ss, rs, extra, act):
        @pl.when((pp >= PL - W) & has_up & extra)
        def _():
            act(z_copy(ext, pp, True, ss, rs))

        @pl.when((pp < W) & has_dn & extra)
        def _():
            act(z_copy(ext, pp, False, ss, rs))

    def start(c):
        c.start()

    def wait_send(c):
        c.wait_send()

    def sib_copy(e):
        ref = k.at[e, own_rows, :]
        return remote(ref, ref, k_sib.at[e], k_recv.at[e], dev(sib, s))

    always = p >= 0
    for t in range(L):
        y_copy(st_ref.at[0], b, t, b_ysend, b_recv).start()
    for t in range(L):
        b[W + h * L + t, own_rows, :] = st_ref[0, t, pl.ds(own_src, RW), :]
    for t in range(L):
        z_each(b, h * L + t, b_zsend, b_recv, always, start)

    S_EY = quarter((NY, YC), 0)
    S_EYT = quarter((YC, NY), 1)
    S_EZ = quarter((NZ, LANES), 0)
    S_EZT = quarter((LANES, NZ), 1)
    scale = 1.0 / FACTOR**3

    def cond_plane(t):
        m = mat_ref[t]
        c = jnp.zeros((NY, NZ), jnp.float32)
        for region in range(regions):
            c = jnp.where(m == region, cond_ref[region], c)
        k_slab[t] = jnp.sqrt(c)
        return c

    for lc in range(LC):
        def body(j, acc, lc=lc):
            return acc + cond_plane(lc * FACTOR + j)

        csum = lax.fori_loop(0, FACTOR, body, jnp.zeros((NY, NZ), jnp.float32))
        gath[s, LC + lc] = mm(mm(S_EYT, csum), S_EZ) * scale
    for t in range(L):
        @pl.when(par == t % 2)
        def _(t=t):
            y_copy(k_slab, k, t, k_ysend, k_recv).start()
    for t in range(L):
        k[W + h * L + t, own_rows, :] = k_slab[t, pl.ds(own_src, RW), :]
    for t in range(L):
        z_each(k, h * L + t, k_zsend, k_recv, par == t % 2, start)

    for lc in range(LC):
        ssum = st_ref[0, lc * FACTOR]
        for j in range(1, FACTOR):
            ssum = ssum + st_ref[0, lc * FACTOR + j]
        gath[s, lc] = mm(mm(S_EYT, ssum), S_EZ) * scale

    def peer_copies(ref_of, ss, rs):
        sends, recvs = [], []
        for i in range(1, S):
            to = lax.rem(s + i, S)
            fr = lax.rem(s + S - i, S)
            sends.append(remote(ref_of(s), ref_of(s), ss.at[i], rs.at[i], dev(tm, to)))
            recvs.append(remote(ref_of(fr), ref_of(fr), ss.at[i], rs.at[i], dev(tm, to)))
        return sends, recvs

    gs, gr = peer_copies(lambda j: gath.at[j], g_send, g_recv)
    for c in gs:
        c.start()

    for ext in (b, k):
        for e in range(E):
            ext[e, zero_rows, :] = jnp.zeros((RH, NZ), jnp.float32)

    @pl.when(jnp.logical_not(has_dn))
    def _():
        for ext in (b, k):
            for e in range(W):
                ext[e, own_rows, :] = jnp.zeros((RW, NZ), jnp.float32)

    @pl.when(jnp.logical_not(has_up))
    def _():
        for ext in (b, k):
            for e in range(W + PL, E):
                ext[e, own_rows, :] = jnp.zeros((RW, NZ), jnp.float32)

    for t in range(L):
        pp = (1 - h) * L + t
        plane_recv(b, W + pp, b_ysend.at[t], b_recv).wait_recv()
        z_each(b, pp, b_zsend, b_recv, always, start)
    for t in range(L):
        pp = (1 - h) * L + t

        @pl.when(par == t % 2)
        def _(t=t, pp=pp):
            plane_recv(k, W + pp, k_ysend.at[t], k_recv).wait_recv()
            z_each(k, pp, k_zsend, k_recv, always, start)
            sib_copy(W + pp).start()

    for c in gr:
        c.wait_recv()

    def coarse_of(first):
        return jnp.concatenate([gath[j, first:first + LC] for j in range(S)], axis=0)

    K = coarse_of(LC)
    shape = (XC, YC, LANES)
    row = lax.broadcasted_iota(jnp.int32, shape, 1)
    lane = lax.broadcasted_iota(jnp.int32, shape, 2)
    pad = lane >= ZC

    def moved(a):
        return (
            jnp.concatenate([a[:1], a[:-1]], axis=0),
            jnp.concatenate([a[1:], a[-1:]], axis=0),
            pltpu.roll(a, 1, 1),
            pltpu.roll(a, YC - 1, 1),
            pltpu.roll(a, 1, 2),
            pltpu.roll(a, LANES - 1, 2),
        )

    plane = lax.broadcasted_iota(jnp.int32, shape, 0)
    edges = (plane == 0, plane == XC - 1, row == 0, row == YC - 1, lane == 0, lane == ZC - 1)
    diag = jnp.ones(shape, jnp.float32)
    for i, (near, edge) in enumerate(zip(moved(K), edges)):
        coef = 0.15 * (K + jnp.where(edge, K, near))
        diag = diag + coef
        coefs[i] = jnp.where(edge | pad, 0.0, coef)
    rdiag[...] = 1.0 / diag

    halo = [(e, has_dn, (e + PL - W) % 2) for e in range(W)]
    halo += [(e, has_up, (e - PL - W) % 2) for e in range(W + PL, E)]
    for e, has, _ in halo:
        @pl.when(has)
        def _(e=e):
            plane_recv(b, e, b_ysend.at[0], b_recv).wait_recv()
    for e, has, parity in halo:
        @pl.when(has & (par == parity))
        def _(e=e):
            plane_recv(k, e, k_ysend.at[0], k_recv).wait_recv()
            sib_copy(e).start()
    for t in range(L):
        @pl.when(par != t % 2)
        def _(t=t):
            plane_recv(k, W + (1 - h) * L + t, k_ysend.at[t], k_recv).wait_recv()
    for e, has, parity in halo:
        @pl.when(has & (par != parity))
        def _(e=e):
            plane_recv(k, e, k_ysend.at[0], k_recv).wait_recv()

    lane2 = lax.broadcasted_iota(jnp.int32, (RE, NZ), 1)

    def stencil(u, e):
        c = u[e]
        w = u[e - 1] + u[e + 1] + (c + c)
        w = (w + w) + pltpu.roll(w, 1, 0) + pltpu.roll(w, RE - 1, 0)
        left = jnp.where(lane2 == 0, 0.0, pltpu.roll(w, 1, 1))
        right = jnp.where(lane2 == NZ - 1, 0.0, pltpu.roll(w, NZ - 1, 1))
        t = (w + w) + (left + right)
        return 2.4 * c - 0.0375 * t

    def inner(v):
        return jnp.sum(v[RH:RH + HY].reshape(HY // 8, 8, NZ), axis=0)

    def weight(e):
        return jnp.where((e >= W) & (e < W + PL), 1.0, 0.0)

    acc0 = jnp.zeros((8, NZ), jnp.float32)

    def moments(u0, u1, lo):
        def pass1(e, m0):
            kk = k[e]
            rr = -(kk * stencil(u0, e))
            r[e] = rr
            u1[e] = kk * rr
            return m0 + weight(e) * inner(rr * rr)

        m0 = lax.fori_loop(lo, E - lo, pass1, acc0)

        def pass2(e, m):
            kk = k[e]
            rr = r[e]
            qq = rr + kk * stencil(u1, e)
            q[e] = qq
            u0[e] = kk * qq
            return m[0] + weight(e) * inner(rr * qq), m[1] + weight(e) * inner(qq * qq)

        m1, m2 = lax.fori_loop(lo + 1, E - lo - 1, pass2, (acc0, acc0))

        def pass3(e, m3):
            return m3 + inner(u0[e] * stencil(u0, e))

        m3 = lax.fori_loop(W, W + PL, pass3, m2)
        return m0, m1, m2, m3

    def scalars(ms, g):
        rows = []
        for m in ms:
            v = jnp.sum(m, axis=0, keepdims=True)
            w = v[:, :LANES]
            for i in range(1, NZ // LANES):
                w = w + v[:, i * LANES:(i + 1) * LANES]
            rows.append(w)
        rows.append(jnp.zeros((4, LANES), jnp.float32))
        red[g, s] = jnp.concatenate(rows, axis=0)
        sends, recvs = peer_copies(lambda j: red.at[g, j], a_send.at[g], a_recv.at[g])
        for c in sends:
            c.start()
        for c in recvs:
            c.wait_recv()
        tot = red[g, 0]
        for j in range(1, S):
            tot = tot + red[g, j]
        tot = jnp.sum(tot, axis=1, keepdims=True)
        m0, m1, m2, m3 = (tot[i:i + 1] for i in range(4))
        a0 = m0 / m1
        rr1 = m0 - 2.0 * a0 * m1 + a0 * a0 * m2
        g1 = 1.0 + rr1 / m0
        curv = g1 * g1 * m1 - 2.0 * g1 * a0 * m2 + a0 * a0 * m3
        a1 = rr1 / curv
        return a0 + a1 * g1, -(a1 * a0), sends

    def first(e, _):
        ua[e] = k[e] * b[e]
        return 0

    lax.fori_loop(0, E, first, 0)
    c1, c2, sends1 = scalars(moments(ua, ub, 1), 0)

    def update(e, _):
        x = b[e] + c1 * r[e] + c2 * q[e]
        b[e] = x
        ua[e] = k[e] * x
        return 0

    for t in range(L):
        y_copy(st_ref.at[0], b, t, b_ysend, b_recv).wait_send()
    for pp in range(PL):
        z_each(b, pp, b_zsend, b_recv, always, wait_send)
    lax.fori_loop(2, E - 2, update, 0)
    c1, c2, sends2 = scalars(moments(ua, ub, 3), 1)

    rows_in = slice(RH, RH + HY)
    for pc in range(PL // FACTOR):
        def last(j, acc, pc=pc):
            i = pc * FACTOR + j
            e = W + i
            x = b[e, rows_in, :] + c1 * r[e, rows_in, :] + c2 * q[e, rows_in, :]
            xf[i] = x
            return acc + x

        xsum = lax.fori_loop(0, FACTOR, last, jnp.zeros((HY, NZ), jnp.float32))
        ey = quarter((HY // FACTOR, HY), 1)
        ce[s, pc] = mm(mm(ey, xsum), S_EZ) * scale

    cs, cr = peer_copies(lambda j: ce.at[j], c_send, c_recv)
    for c in cs:
        c.start()

    def end_copy(same):
        half = h if same else 1 - h
        to = s if same else partner
        i = 0 if same else 1
        rows = pl.ds(pl.multiple_of(h * HY, 8), HY)
        return remote(
            xf.at[pl.ds(half * L, L)], fe.at[:, rows, :], e_send.at[i], e_recv.at[i], dev(tm + 1, to)
        )

    def end_recv(same):
        src_half = h if same else 1 - h
        i = 0 if same else 1
        ref = fe.at[:, pl.ds(pl.multiple_of(src_half * HY, 8), HY), :]
        return remote(ref, ref, e_send.at[i], e_recv.at[i], dev(tm - 1, s))

    has_next = tm < T - 1

    @pl.when(has_next)
    def _():
        end_copy(False).start()
        end_copy(True).start()

    for c in cr:
        c.wait_recv()

    HC = HY // FACTOR
    for j in range(S):
        path_ref[0, (j // 2) * 2 * LC:(j // 2 + 1) * 2 * LC, (j % 2) * HC:(j % 2 + 1) * HC, :] = ce[j, :, :, :ZC]

    def relay_path():
        return remote(pout, pin, p_send.at[0], p_recv.at[0], dev(tm + 1, s))

    pout = coefs.at[6]

    def relay_d():
        return remote(dsend, din, p_send.at[1], p_recv.at[1], dev(tm + 1, s))

    def ce_full():
        blocks = []
        for j in range(0, S, 2):
            blocks.append(jnp.concatenate([ce[j], ce[j + 1]], axis=1))
        return jnp.concatenate(blocks, axis=0)

    @pl.when(tm == 0)
    def _():
        pout[...] = ce_full()
        dsend[...] = jnp.zeros((LC, YC, LANES), jnp.float32)

    @pl.when(tm > 0)
    def _():
        remote(pin, pin, p_send.at[0], p_recv.at[0], dev(tm - 1, s)).wait_recv()
        remote(din, din, p_send.at[1], p_recv.at[1], dev(tm - 1, s)).wait_recv()
        src = pin[...] - coarse_of(0)
        w = src
        for _i in range(JACOBI):
            acc = src
            for i, near in enumerate(moved(w)):
                acc = acc + coefs[i] * near
            w = acc * rdiag[...]
        pout[...] = w
        dsend[...] = coefs[6, pl.ds(s * LC, LC)]
        pth = w + ce_full()
        pout[...] = pth
        path_ref[0] = pth[:, :, :ZC]

    @pl.when(has_next)
    def _():
        relay_path().start()
        relay_d().start()

    @pl.when(tm == 0)
    def _():
        out_ref[...] = st_ref[...]

    @pl.when(tm > 0)
    def _():
        end_recv(True).wait_recv()
        end_recv(False).wait_recv()
        for lc in range(LC):
            up = mm(mm(S_EY, din[lc]), S_EZT)
            for j in range(FACTOR):
                i = lc * FACTOR + j
                out_ref[0, i] = fe[i] + up

    for t in range(L):
        @pl.when(par == t % 2)
        def _(t=t):
            y_copy(k_slab, k, t, k_ysend, k_recv).wait_send()
            sib_copy(W + (1 - h) * L + t).wait_send()
    for pp in range(PL):
        z_each(k, pp, k_zsend, k_recv, par == pp % 2, wait_send)
    for e, has, parity in halo:
        @pl.when(has & (par == parity))
        def _(e=e):
            sib_copy(e).wait_send()
    for c in gs + sends1 + sends2 + cs:
        c.wait_send()

    @pl.when(has_next)
    def _():
        end_copy(False).wait_send()
        end_copy(True).wait_send()
        relay_path().wait_send()
        relay_d().wait_send()


def local(T, S, starts, material, conductivity):
    _, L, NY, NZ = starts.shape
    E = 2 * L + 2 * W
    HY = NY // 2
    RE = HY + 2 * RH
    LC = L // FACTOR
    XC, YC, ZC = LC * S, NY // FACTOR, NZ // FACTOR
    f32 = jnp.float32
    ext = pltpu.VMEM((E, RE, NZ), f32)
    dma = pltpu.SemaphoreType.DMA
    vm = pl.BlockSpec(memory_space=pltpu.VMEM)
    return pl.pallas_call(
        functools.partial(kernel, T, S, L, NY, NZ, conductivity.shape[0]),
        out_shape=(
            jax.ShapeDtypeStruct(starts.shape, f32),
            jax.ShapeDtypeStruct((1, XC, YC, ZC), f32),
        ),
        in_specs=[pl.BlockSpec(memory_space=pltpu.SMEM), vm, vm],
        out_specs=(vm, vm),
        scratch_shapes=[
            pltpu.VMEM((L, NY, NZ), f32), ext, ext, ext, ext, ext, ext,
            pltpu.VMEM((2 * L, HY, NZ), f32), pltpu.VMEM((L, NY, NZ), f32),
            pltpu.VMEM((2, S, 8, LANES), f32),
            pltpu.VMEM((S, 2 * LC, YC, LANES), f32),
            pltpu.VMEM((S, 2 * LC, YC // 2, LANES), f32),
            pltpu.VMEM((XC, YC, LANES), f32),
            pltpu.VMEM((LC, YC, LANES), f32),
            pltpu.VMEM((LC, YC, LANES), f32),
            pltpu.VMEM((7, XC, YC, LANES), f32),
            pltpu.VMEM((XC, YC, LANES), f32),
            dma((E,)), dma((E,)), dma((L,)), dma((L,)), dma((2, 2 * L)), dma((2, 2 * L)), dma((E,)),
            dma((2, S)), dma((2, S)), dma((S,)), dma((S,)), dma((S,)), dma((S,)),
            dma((2,)), dma((2,)), dma((2,)), dma((2,)),
        ],
        compiler_params=pltpu.CompilerParams(
            collective_id=0, has_side_effects=True, vmem_limit_bytes=60 * 1024 * 1024
        ),
    )(conductivity, starts, material)


def solution(mesh):
    return jax.shard_map(
        functools.partial(local, mesh.shape["tm"], mesh.shape["space"]),
        mesh=mesh,
        in_specs=(P("tm", "space", None, None), P("space", None, None), P()),
        out_specs=(P("tm", "space", None, None), P("tm", None, None, None)),
        check_vma=False,
    )
```

```python
import functools

import jax
import jax.numpy as jnp
from jax import lax
from jax.experimental import pallas as pl
from jax.experimental.pallas import tpu as pltpu
from jax.sharding import PartitionSpec as P

FACTOR = 4
JACOBI = 3
W = 5
RH = 8
LANES = 128
HIGH = lax.Precision.HIGHEST
MESH = pl.DeviceIdType.MESH


def quarter(shape, long_axis):
    fine = lax.shift_right_logical(lax.broadcasted_iota(jnp.int32, shape, long_axis), 2)
    coarse = lax.broadcasted_iota(jnp.int32, shape, 1 - long_axis)
    return jnp.where(fine == coarse, 1.0, 0.0).astype(jnp.float32)


def mm(a, b):
    return jnp.dot(a, b, precision=HIGH, preferred_element_type=jnp.float32)


def kernel(
    T, S, L, NY, NZ, regions,
    cond_ref, st_ref, mat_ref,
    out_ref, path_ref,
    k_slab, b, k, ua, ub, r, q, xf, fe,
    red, gath, ce, pin, din, dsend, coefs, rdiag,
    b_recv, k_recv, b_ysend, k_ysend, b_zsend, k_zsend, k_sib,
    a_send, a_recv, g_send, g_recv, c_send, c_recv, e_send, e_recv, p_send, p_recv,
):
    tm = lax.axis_index("tm")
    s = lax.axis_index("space")
    h = lax.rem(s, 2)
    p = s // 2
    NP = S // 2
    PL = 2 * L
    E = PL + 2 * W
    HY = NY // 2
    RW = HY + RH
    RE = HY + 2 * RH
    partner = s + 1 - 2 * h
    par = lax.rem(tm, 2)
    sib = tm + 1 - 2 * par
    has_up = p < NP - 1
    has_dn = p > 0
    LC = L // FACTOR
    XC = LC * S
    YC = NY // FACTOR
    ZC = NZ // FACTOR

    def dev(t_, s_):
        return (t_, s_)

    def remote(src, dst, ss, rs, d):
        return pltpu.make_async_remote_copy(
            src_ref=src, dst_ref=dst, send_sem=ss, recv_sem=rs, device_id=d, device_id_type=MESH
        )

    own_off = pl.multiple_of(RH - RH * h, 8)
    own_src = pl.multiple_of((HY - RH) * h, 8)
    oth_off = pl.multiple_of(RH * h, 8)
    oth_src = pl.multiple_of((HY - RH) * (1 - h), 8)
    own_rows = pl.ds(own_off, RW)
    zero_rows = pl.ds(pl.multiple_of(h * RW, 8), RH)

    bar = pltpu.get_barrier_semaphore()
    for i in range(1, S):
        pl.semaphore_signal(bar, 1, device_id=dev(tm, lax.rem(s + i, S)), device_id_type=MESH)

    @pl.when(tm < T - 1)
    def _():
        pl.semaphore_signal(bar, 1, device_id=dev(tm + 1, s), device_id_type=MESH)
        pl.semaphore_signal(bar, 1, device_id=dev(tm + 1, partner), device_id_type=MESH)

    @pl.when(tm > 0)
    def _():
        pl.semaphore_signal(bar, 1, device_id=dev(tm - 1, s), device_id_type=MESH)
        pl.semaphore_signal(bar, 1, device_id=dev(tm - 1, partner), device_id_type=MESH)

    tm_peers = 2 * jnp.where(tm < T - 1, 1, 0) + 2 * jnp.where(tm > 0, 1, 0)
    pl.semaphore_wait(bar, S - 1 + tm_peers)

    def y_copy(slab, ext, t, ss, rs):
        e = W + h * L + t
        return remote(
            slab.at[t, pl.ds(oth_src, RW), :], ext.at[e, pl.ds(oth_off, RW), :],
            ss.at[t], rs.at[e], dev(tm, partner),
        )

    def plane_recv(ext, e, ss, rs):
        ref = ext.at[e, own_rows, :]
        return remote(ref, ref, ss, rs.at[e], dev(tm, partner))

    def z_copy(ext, pp, up, ss, rs):
        src = ext.at[W + pp, own_rows, :]
        if up:
            e = pp - PL + W
            return remote(src, ext.at[e, own_rows, :], ss.at[0, pp], rs.at[e], dev(tm, s + 2))
        e = pp + PL + W
        return remote(src, ext.at[e, own_rows, :], ss.at[1, pp], rs.at[e], dev(tm, s - 2))

    def z_each(ext, pp, ss, rs, extra, act):
        @pl.when((pp >= PL - W) & has_up & extra)
        def _():
            act(z_copy(ext, pp, True, ss, rs))

        @pl.when((pp < W) & has_dn & extra)
        def _():
            act(z_copy(ext, pp, False, ss, rs))

    def start(c):
        c.start()

    def wait_send(c):
        c.wait_send()

    def sib_copy(e):
        ref = k.at[e, own_rows, :]
        return remote(ref, ref, k_sib.at[e], k_recv.at[e], dev(sib, s))

    always = p >= 0
    for t in range(L):
        y_copy(st_ref.at[0], b, t, b_ysend, b_recv).start()
    for t in range(L):
        b[W + h * L + t, own_rows, :] = st_ref[0, t, pl.ds(own_src, RW), :]
    for t in range(L):
        z_each(b, h * L + t, b_zsend, b_recv, always, start)

    S_EY = quarter((NY, YC), 0)
    S_EYT = quarter((YC, NY), 1)
    S_EZ = quarter((NZ, LANES), 0)
    S_EZT = quarter((LANES, NZ), 1)
    scale = 1.0 / FACTOR**3

    def cond_plane(t):
        m = mat_ref[t]
        c = jnp.zeros((NY, NZ), jnp.float32)
        for region in range(regions):
            c = jnp.where(m == region, cond_ref[region], c)
        k_slab[t] = jnp.sqrt(c)
        return c

    for lc in range(LC):
        def body(j, acc, lc=lc):
            return acc + cond_plane(lc * FACTOR + j)

        csum = lax.fori_loop(0, FACTOR, body, jnp.zeros((NY, NZ), jnp.float32))
        gath[s, LC + lc] = mm(mm(S_EYT, csum), S_EZ) * scale
    for t in range(L):
        @pl.when(par == t % 2)
        def _(t=t):
            y_copy(k_slab, k, t, k_ysend, k_recv).start()
    for t in range(L):
        k[W + h * L + t, own_rows, :] = k_slab[t, pl.ds(own_src, RW), :]
    for t in range(L):
        z_each(k, h * L + t, k_zsend, k_recv, par == t % 2, start)

    for lc in range(LC):
        ssum = st_ref[0, lc * FACTOR]
        for j in range(1, FACTOR):
            ssum = ssum + st_ref[0, lc * FACTOR + j]
        gath[s, lc] = mm(mm(S_EYT, ssum), S_EZ) * scale

    def peer_copies(ref_of, ss, rs):
        sends, recvs = [], []
        for i in range(1, S):
            to = lax.rem(s + i, S)
            fr = lax.rem(s + S - i, S)
            sends.append(remote(ref_of(s), ref_of(s), ss.at[i], rs.at[i], dev(tm, to)))
            recvs.append(remote(ref_of(fr), ref_of(fr), ss.at[i], rs.at[i], dev(tm, to)))
        return sends, recvs

    gs, gr = peer_copies(lambda j: gath.at[j], g_send, g_recv)

    for ext in (b, k):
        for e in range(E):
            ext[e, zero_rows, :] = jnp.zeros((RH, NZ), jnp.float32)

    @pl.when(jnp.logical_not(has_dn))
    def _():
        for ext in (b, k):
            for e in range(W):
                ext[e, own_rows, :] = jnp.zeros((RW, NZ), jnp.float32)

    @pl.when(jnp.logical_not(has_up))
    def _():
        for ext in (b, k):
            for e in range(W + PL, E):
                ext[e, own_rows, :] = jnp.zeros((RW, NZ), jnp.float32)

    for t in range(L):
        pp = (1 - h) * L + t
        plane_recv(b, W + pp, b_ysend.at[t], b_recv).wait_recv()
        z_each(b, pp, b_zsend, b_recv, always, start)
    for t in range(L):
        pp = (1 - h) * L + t

        @pl.when(par == t % 2)
        def _(t=t, pp=pp):
            plane_recv(k, W + pp, k_ysend.at[t], k_recv).wait_recv()
            z_each(k, pp, k_zsend, k_recv, always, start)
            sib_copy(W + pp).start()

    for c in gs:
        c.start()
    for t in range(L):
        @pl.when(par != t % 2)
        def _(t=t):
            plane_recv(k, W + (1 - h) * L + t, k_ysend.at[t], k_recv).wait_recv()

    lane2 = lax.broadcasted_iota(jnp.int32, (RE, NZ), 1)

    def stencil(u, e):
        c = u[e]
        w = u[e - 1] + u[e + 1] + (c + c)
        w = (w + w) + pltpu.roll(w, 1, 0) + pltpu.roll(w, RE - 1, 0)
        left = jnp.where(lane2 == 0, 0.0, pltpu.roll(w, 1, 1))
        right = jnp.where(lane2 == NZ - 1, 0.0, pltpu.roll(w, NZ - 1, 1))
        t = (w + w) + (left + right)
        return 2.4 * c - 0.0375 * t

    def inner(v):
        return jnp.sum(v[RH:RH + HY].reshape(HY // 8, 8, NZ), axis=0)

    def weight(e):
        return jnp.where((e >= W) & (e < W + PL), 1.0, 0.0)

    acc0 = jnp.zeros((8, NZ), jnp.float32)

    def passes(u0, u1):
        def pass1(e, m0):
            kk = k[e]
            rr = -(kk * stencil(u0, e))
            r[e] = rr
            u1[e] = kk * rr
            return m0 + weight(e) * inner(rr * rr)

        def pass2(e, m):
            kk = k[e]
            rr = r[e]
            qq = rr + kk * stencil(u1, e)
            q[e] = qq
            u0[e] = kk * qq
            return m[0] + weight(e) * inner(rr * qq), m[1] + weight(e) * inner(qq * qq)

        def pass3(e, m3):
            return m3 + inner(u0[e] * stencil(u0, e))

        return pass1, pass2, pass3

    def scalars(ms, g, beside=None):
        rows = []
        for m in ms:
            v = jnp.sum(m, axis=0, keepdims=True)
            w = v[:, :LANES]
            for i in range(1, NZ // LANES):
                w = w + v[:, i * LANES:(i + 1) * LANES]
            rows.append(w)
        rows.append(jnp.zeros((4, LANES), jnp.float32))
        red[g, s] = jnp.concatenate(rows, axis=0)
        sends, recvs = peer_copies(lambda j: red.at[g, j], a_send.at[g], a_recv.at[g])
        for c in sends:
            c.start()
        if beside is not None:
            beside()
        for c in recvs:
            c.wait_recv()
        tot = red[g, 0]
        for j in range(1, S):
            tot = tot + red[g, j]
        tot = jnp.sum(tot, axis=1, keepdims=True)
        m0, m1, m2, m3 = (tot[i:i + 1] for i in range(4))
        a0 = m0 / m1
        rr1 = m0 - 2.0 * a0 * m1 + a0 * a0 * m2
        g1 = 1.0 + rr1 / m0
        curv = g1 * g1 * m1 - 2.0 * g1 * a0 * m2 + a0 * a0 * m3
        a1 = rr1 / curv
        return a0 + a1 * g1, -(a1 * a0), sends

    def first(e, _):
        ua[e] = k[e] * b[e]
        return 0

    pass1, pass2, pass3 = passes(ua, ub)
    lax.fori_loop(W, W + PL, first, 0)
    m0 = lax.fori_loop(W + 1, W + PL - 1, pass1, acc0)
    m12 = lax.fori_loop(W + 2, W + PL - 2, pass2, (acc0, acc0))

    halo = [(e, has_dn, (e + PL - W) % 2) for e in range(W)]
    halo += [(e, has_up, (e - PL - W) % 2) for e in range(W + PL, E)]
    for e, has, _ in halo:
        @pl.when(has)
        def _(e=e):
            plane_recv(b, e, b_ysend.at[0], b_recv).wait_recv()
    for e, has, parity in halo:
        @pl.when(has & (par == parity))
        def _(e=e):
            plane_recv(k, e, k_ysend.at[0], k_recv).wait_recv()
            sib_copy(e).start()
    for e, has, parity in halo:
        @pl.when(has & (par != parity))
        def _(e=e):
            plane_recv(k, e, k_ysend.at[0], k_recv).wait_recv()

    lax.fori_loop(0, W, first, 0)
    lax.fori_loop(W + PL, E, first, 0)
    m0 = lax.fori_loop(1, W + 1, pass1, m0)
    m0 = lax.fori_loop(W + PL - 1, E - 1, pass1, m0)
    m12 = lax.fori_loop(2, W + 2, pass2, m12)
    m12 = lax.fori_loop(W + PL - 2, E - 2, pass2, m12)
    m3 = lax.fori_loop(W, W + PL, pass3, m12[1])
    c1, c2, sends1 = scalars((m0,) + m12 + (m3,), 0)

    def update(e, _):
        x = b[e] + c1 * r[e] + c2 * q[e]
        b[e] = x
        ua[e] = k[e] * x
        return 0

    for t in range(L):
        y_copy(st_ref.at[0], b, t, b_ysend, b_recv).wait_send()
    for pp in range(PL):
        z_each(b, pp, b_zsend, b_recv, always, wait_send)
    lax.fori_loop(2, E - 2, update, 0)
    def coarse_of(first):
        return jnp.concatenate([gath[j, first:first + LC] for j in range(S)], axis=0)

    def moved(a):
        return (
            jnp.concatenate([a[:1], a[:-1]], axis=0),
            jnp.concatenate([a[1:], a[-1:]], axis=0),
            pltpu.roll(a, 1, 1),
            pltpu.roll(a, YC - 1, 1),
            pltpu.roll(a, 1, 2),
            pltpu.roll(a, LANES - 1, 2),
        )

    def coarse_setup():
        for c in gr:
            c.wait_recv()

        K = coarse_of(LC)
        shape = (XC, YC, LANES)
        row = lax.broadcasted_iota(jnp.int32, shape, 1)
        lane = lax.broadcasted_iota(jnp.int32, shape, 2)
        pad = lane >= ZC

        plane = lax.broadcasted_iota(jnp.int32, shape, 0)
        edges = (plane == 0, plane == XC - 1, row == 0, row == YC - 1, lane == 0, lane == ZC - 1)
        diag = jnp.ones(shape, jnp.float32)
        for i, (near, edge) in enumerate(zip(moved(K), edges)):
            coef = 0.15 * (K + jnp.where(edge, K, near))
            diag = diag + coef
            coefs[i] = jnp.where(edge | pad, 0.0, coef)
        rdiag[...] = 1.0 / diag

    m0 = lax.fori_loop(3, E - 3, pass1, acc0)
    m12 = lax.fori_loop(4, E - 4, pass2, (acc0, acc0))
    m3 = lax.fori_loop(W, W + PL, pass3, m12[1])
    c1, c2, sends2 = scalars((m0,) + m12 + (m3,), 1, coarse_setup)

    rows_in = slice(RH, RH + HY)
    for pc in range(PL // FACTOR):
        def last(j, acc, pc=pc):
            i = pc * FACTOR + j
            e = W + i
            x = b[e, rows_in, :] + c1 * r[e, rows_in, :] + c2 * q[e, rows_in, :]
            xf[i] = x
            return acc + x

        xsum = lax.fori_loop(0, FACTOR, last, jnp.zeros((HY, NZ), jnp.float32))
        ey = quarter((HY // FACTOR, HY), 1)
        ce[s, pc] = mm(mm(ey, xsum), S_EZ) * scale

    cs, cr = peer_copies(lambda j: ce.at[j], c_send, c_recv)
    for c in cs:
        c.start()

    def end_copy(same):
        half = h if same else 1 - h
        to = s if same else partner
        i = 0 if same else 1
        rows = pl.ds(pl.multiple_of(h * HY, 8), HY)
        return remote(
            xf.at[pl.ds(half * L, L)], fe.at[:, rows, :], e_send.at[i], e_recv.at[i], dev(tm + 1, to)
        )

    def end_recv(same):
        src_half = h if same else 1 - h
        i = 0 if same else 1
        ref = fe.at[:, pl.ds(pl.multiple_of(src_half * HY, 8), HY), :]
        return remote(ref, ref, e_send.at[i], e_recv.at[i], dev(tm - 1, s))

    has_next = tm < T - 1

    @pl.when(has_next)
    def _():
        end_copy(False).start()

    for c in cr:
        c.wait_recv()

    HC = HY // FACTOR
    for j in range(S):
        path_ref[0, (j // 2) * 2 * LC:(j // 2 + 1) * 2 * LC, (j % 2) * HC:(j % 2 + 1) * HC, :] = ce[j, :, :, :ZC]

    def relay_path():
        return remote(pout, pin, p_send.at[0], p_recv.at[0], dev(tm + 1, s))

    pout = coefs.at[6]

    def relay_d():
        return remote(dsend, din, p_send.at[1], p_recv.at[1], dev(tm + 1, s))

    def ce_full():
        blocks = []
        for j in range(0, S, 2):
            blocks.append(jnp.concatenate([ce[j], ce[j + 1]], axis=1))
        return jnp.concatenate(blocks, axis=0)

    @pl.when(tm == 0)
    def _():
        pout[...] = ce_full()
        dsend[...] = jnp.zeros((LC, YC, LANES), jnp.float32)

    @pl.when(tm > 0)
    def _():
        remote(pin, pin, p_send.at[0], p_recv.at[0], dev(tm - 1, s)).wait_recv()
        remote(din, din, p_send.at[1], p_recv.at[1], dev(tm - 1, s)).wait_recv()
        src = pin[...] - coarse_of(0)
        w = src
        for _i in range(JACOBI):
            acc = src
            for i, near in enumerate(moved(w)):
                acc = acc + coefs[i] * near
            w = acc * rdiag[...]
        pout[...] = w
        dsend[...] = coefs[6, pl.ds(s * LC, LC)]
        pth = w + ce_full()
        pout[...] = pth
        path_ref[0] = pth[:, :, :ZC]

    @pl.when(has_next)
    def _():
        relay_path().start()
        relay_d().start()
        end_copy(True).start()

    @pl.when(tm == 0)
    def _():
        out_ref[...] = st_ref[...]

    @pl.when(tm > 0)
    def _():
        end_recv(True).wait_recv()
        end_recv(False).wait_recv()
        for lc in range(LC):
            up = mm(mm(S_EY, din[lc]), S_EZT)
            for j in range(FACTOR):
                i = lc * FACTOR + j
                out_ref[0, i] = fe[i] + up

    for t in range(L):
        @pl.when(par == t % 2)
        def _(t=t):
            y_copy(k_slab, k, t, k_ysend, k_recv).wait_send()
            sib_copy(W + (1 - h) * L + t).wait_send()
    for pp in range(PL):
        z_each(k, pp, k_zsend, k_recv, par == pp % 2, wait_send)
    for e, has, parity in halo:
        @pl.when(has & (par == parity))
        def _(e=e):
            sib_copy(e).wait_send()
    for c in gs + sends1 + sends2 + cs:
        c.wait_send()

    @pl.when(has_next)
    def _():
        end_copy(False).wait_send()
        end_copy(True).wait_send()
        relay_path().wait_send()
        relay_d().wait_send()


def local(T, S, starts, material, conductivity):
    _, L, NY, NZ = starts.shape
    E = 2 * L + 2 * W
    HY = NY // 2
    RE = HY + 2 * RH
    LC = L // FACTOR
    XC, YC, ZC = LC * S, NY // FACTOR, NZ // FACTOR
    f32 = jnp.float32
    ext = pltpu.VMEM((E, RE, NZ), f32)
    dma = pltpu.SemaphoreType.DMA
    vm = pl.BlockSpec(memory_space=pltpu.VMEM)
    return pl.pallas_call(
        functools.partial(kernel, T, S, L, NY, NZ, conductivity.shape[0]),
        out_shape=(
            jax.ShapeDtypeStruct(starts.shape, f32),
            jax.ShapeDtypeStruct((1, XC, YC, ZC), f32),
        ),
        in_specs=[pl.BlockSpec(memory_space=pltpu.SMEM), vm, vm],
        out_specs=(vm, vm),
        scratch_shapes=[
            pltpu.VMEM((L, NY, NZ), f32), ext, ext, ext, ext, ext, ext,
            pltpu.VMEM((2 * L, HY, NZ), f32), pltpu.VMEM((L, NY, NZ), f32),
            pltpu.VMEM((2, S, 8, LANES), f32),
            pltpu.VMEM((S, 2 * LC, YC, LANES), f32),
            pltpu.VMEM((S, 2 * LC, YC // 2, LANES), f32),
            pltpu.VMEM((XC, YC, LANES), f32),
            pltpu.VMEM((LC, YC, LANES), f32),
            pltpu.VMEM((LC, YC, LANES), f32),
            pltpu.VMEM((7, XC, YC, LANES), f32),
            pltpu.VMEM((XC, YC, LANES), f32),
            dma((E,)), dma((E,)), dma((L,)), dma((L,)), dma((2, 2 * L)), dma((2, 2 * L)), dma((E,)),
            dma((2, S)), dma((2, S)), dma((S,)), dma((S,)), dma((S,)), dma((S,)),
            dma((2,)), dma((2,)), dma((2,)), dma((2,)),
        ],
        compiler_params=pltpu.CompilerParams(
            collective_id=0, has_side_effects=True, vmem_limit_bytes=60 * 1024 * 1024
        ),
    )(conductivity, starts, material)


def solution(mesh):
    return jax.shard_map(
        functools.partial(local, mesh.shape["tm"], mesh.shape["space"]),
        mesh=mesh,
        in_specs=(P("tm", "space", None, None), P("space", None, None), P()),
        out_specs=(P("tm", "space", None, None), P("tm", None, None, None)),
        check_vma=False,
    )
```

```python
import functools

import jax
import jax.numpy as jnp
from jax import lax
from jax.experimental import pallas as pl
from jax.experimental.pallas import tpu as pltpu
from jax.sharding import PartitionSpec as P

FACTOR = 4
JACOBI = 3
W = 5
RH = 8
LANES = 128
HIGH = lax.Precision.HIGHEST
MESH = pl.DeviceIdType.MESH


def quarter(shape, long_axis):
    fine = lax.shift_right_logical(lax.broadcasted_iota(jnp.int32, shape, long_axis), 2)
    coarse = lax.broadcasted_iota(jnp.int32, shape, 1 - long_axis)
    return jnp.where(fine == coarse, 1.0, 0.0).astype(jnp.float32)


def mm(a, b):
    return jnp.dot(a, b, precision=HIGH, preferred_element_type=jnp.float32)


def kernel(
    T, S, L, NY, NZ, regions,
    cond_ref, st_ref, mat_ref,
    out_ref, path_ref,
    k_slab, b, k, ua, ub, r, q, xf, fe,
    red, gath, ce, pin, din, dsend, coefs, rdiag,
    b_recv, k_recv, b_ysend, k_ysend, b_zsend, k_zsend, k_sib,
    a_send, a_recv, g_send, g_recv, c_send, c_recv, e_send, e_recv, p_send, p_recv,
):
    tm = lax.axis_index("tm")
    s = lax.axis_index("space")
    h = lax.rem(s, 2)
    p = s // 2
    NP = S // 2
    PL = 2 * L
    E = PL + 2 * W
    HY = NY // 2
    RW = HY + RH
    RE = HY + 2 * RH
    partner = s + 1 - 2 * h
    par = lax.rem(tm, 2)
    sib = tm + 1 - 2 * par
    has_up = p < NP - 1
    has_dn = p > 0
    LC = L // FACTOR
    XC = LC * S
    YC = NY // FACTOR
    ZC = NZ // FACTOR

    def dev(t_, s_):
        return (t_, s_)

    def remote(src, dst, ss, rs, d):
        return pltpu.make_async_remote_copy(
            src_ref=src, dst_ref=dst, send_sem=ss, recv_sem=rs, device_id=d, device_id_type=MESH
        )

    own_off = pl.multiple_of(RH - RH * h, 8)
    own_src = pl.multiple_of((HY - RH) * h, 8)
    oth_off = pl.multiple_of(RH * h, 8)
    oth_src = pl.multiple_of((HY - RH) * (1 - h), 8)
    own_rows = pl.ds(own_off, RW)
    zero_rows = pl.ds(pl.multiple_of(h * RW, 8), RH)

    bar = pltpu.get_barrier_semaphore()
    for i in range(1, S):
        pl.semaphore_signal(bar, 1, device_id=dev(tm, lax.rem(s + i, S)), device_id_type=MESH)

    @pl.when(tm < T - 1)
    def _():
        pl.semaphore_signal(bar, 1, device_id=dev(tm + 1, s), device_id_type=MESH)
        pl.semaphore_signal(bar, 1, device_id=dev(tm + 1, partner), device_id_type=MESH)

    @pl.when(tm > 0)
    def _():
        pl.semaphore_signal(bar, 1, device_id=dev(tm - 1, s), device_id_type=MESH)
        pl.semaphore_signal(bar, 1, device_id=dev(tm - 1, partner), device_id_type=MESH)

    tm_peers = 2 * jnp.where(tm < T - 1, 1, 0) + 2 * jnp.where(tm > 0, 1, 0)
    pl.semaphore_wait(bar, S - 1 + tm_peers)

    def y_copy(slab, ext, t, ss, rs):
        e = W + h * L + t
        return remote(
            slab.at[t, pl.ds(oth_src, RW), :], ext.at[e, pl.ds(oth_off, RW), :],
            ss.at[t], rs.at[e], dev(tm, partner),
        )

    def plane_recv(ext, e, ss, rs):
        ref = ext.at[e, own_rows, :]
        return remote(ref, ref, ss, rs.at[e], dev(tm, partner))

    def z_copy(ext, pp, up, ss, rs):
        src = ext.at[W + pp, own_rows, :]
        if up:
            e = pp - PL + W
            return remote(src, ext.at[e, own_rows, :], ss.at[0, pp], rs.at[e], dev(tm, s + 2))
        e = pp + PL + W
        return remote(src, ext.at[e, own_rows, :], ss.at[1, pp], rs.at[e], dev(tm, s - 2))

    def z_each(ext, pp, ss, rs, extra, act):
        @pl.when((pp >= PL - W) & has_up & extra)
        def _():
            act(z_copy(ext, pp, True, ss, rs))

        @pl.when((pp < W) & has_dn & extra)
        def _():
            act(z_copy(ext, pp, False, ss, rs))

    def start(c):
        c.start()

    def wait_send(c):
        c.wait_send()

    def sib_copy(e):
        ref = k.at[e, own_rows, :]
        return remote(ref, ref, k_sib.at[e], k_recv.at[e], dev(sib, s))

    always = p >= 0
    for t in range(L):
        y_copy(st_ref.at[0], b, t, b_ysend, b_recv).start()
    for t in range(L):
        b[W + h * L + t, own_rows, :] = st_ref[0, t, pl.ds(own_src, RW), :]
    for t in range(L):
        z_each(b, h * L + t, b_zsend, b_recv, always, start)

    S_EY = quarter((NY, YC), 0)
    S_EYT = quarter((YC, NY), 1)
    S_EZ = quarter((NZ, LANES), 0)
    S_EZT = quarter((LANES, NZ), 1)
    scale = 1.0 / FACTOR**3

    def cond_plane(t):
        m = mat_ref[t]
        c = jnp.zeros((NY, NZ), jnp.float32)
        for region in range(regions):
            c = jnp.where(m == region, cond_ref[region], c)
        k_slab[t] = jnp.sqrt(c)
        return c

    for lc in range(LC):
        def body(j, acc, lc=lc):
            return acc + cond_plane(lc * FACTOR + j)

        csum = lax.fori_loop(0, FACTOR, body, jnp.zeros((NY, NZ), jnp.float32))
        gath[s, LC + lc] = mm(mm(S_EYT, csum), S_EZ) * scale
    for t in range(L):
        @pl.when(par == t % 2)
        def _(t=t):
            y_copy(k_slab, k, t, k_ysend, k_recv).start()
    for t in range(L):
        k[W + h * L + t, own_rows, :] = k_slab[t, pl.ds(own_src, RW), :]
    for t in range(L):
        z_each(k, h * L + t, k_zsend, k_recv, par == t % 2, start)

    for lc in range(LC):
        ssum = st_ref[0, lc * FACTOR]
        for j in range(1, FACTOR):
            ssum = ssum + st_ref[0, lc * FACTOR + j]
        gath[s, lc] = mm(mm(S_EYT, ssum), S_EZ) * scale

    def peer_copies(ref_of, ss, rs):
        sends, recvs = [], []
        for i in range(1, S):
            to = lax.rem(s + i, S)
            fr = lax.rem(s + S - i, S)
            sends.append(remote(ref_of(s), ref_of(s), ss.at[i], rs.at[i], dev(tm, to)))
            recvs.append(remote(ref_of(fr), ref_of(fr), ss.at[i], rs.at[i], dev(tm, to)))
        return sends, recvs

    gs, gr = peer_copies(lambda j: gath.at[j], g_send, g_recv)

    for ext in (b, k):
        for e in range(E):
            ext[e, zero_rows, :] = jnp.zeros((RH, NZ), jnp.float32)

    @pl.when(jnp.logical_not(has_dn))
    def _():
        for ext in (b, k):
            for e in range(W):
                ext[e, own_rows, :] = jnp.zeros((RW, NZ), jnp.float32)

    @pl.when(jnp.logical_not(has_up))
    def _():
        for ext in (b, k):
            for e in range(W + PL, E):
                ext[e, own_rows, :] = jnp.zeros((RW, NZ), jnp.float32)

    for t in range(L):
        pp = (1 - h) * L + t
        plane_recv(b, W + pp, b_ysend.at[t], b_recv).wait_recv()
        z_each(b, pp, b_zsend, b_recv, always, start)
    for t in range(L):
        pp = (1 - h) * L + t

        @pl.when(par == t % 2)
        def _(t=t, pp=pp):
            plane_recv(k, W + pp, k_ysend.at[t], k_recv).wait_recv()
            z_each(k, pp, k_zsend, k_recv, always, start)
            sib_copy(W + pp).start()

    for c in gs:
        c.start()
    for t in range(L):
        @pl.when(par != t % 2)
        def _(t=t):
            plane_recv(k, W + (1 - h) * L + t, k_ysend.at[t], k_recv).wait_recv()

    CH = RE // 6 if RE % 48 == 0 else RE
    CHUNKS = range(RE // CH)
    lane2 = lax.broadcasted_iota(jnp.int32, (CH, NZ), 1)

    def part(i):
        return slice(i * CH, (i + 1) * CH)

    def stencil(u, e, i):
        lo, hi = max(0, i * CH - 8), min(RE, (i + 1) * CH + 8)
        rows = slice(lo, hi)
        own = slice(i * CH - lo, i * CH - lo + CH)
        c = u[e, rows]
        w = u[e - 1, rows] + u[e + 1, rows] + (c + c)
        w = ((w + w) + pltpu.roll(w, 1, 0) + pltpu.roll(w, hi - lo - 1, 0))[own]
        left = jnp.where(lane2 == 0, 0.0, pltpu.roll(w, 1, 1))
        right = jnp.where(lane2 == NZ - 1, 0.0, pltpu.roll(w, NZ - 1, 1))
        t = (w + w) + (left + right)
        return 2.4 * c[own] - 0.0375 * t

    def inner(v, i):
        v = v[max(RH - i * CH, 0):min(RH + HY - i * CH, CH)]
        return jnp.sum(v.reshape(v.shape[0] // 8, 8, NZ), axis=0)

    def weight(e):
        return jnp.where((e >= W) & (e < W + PL), 1.0, 0.0)

    acc0 = jnp.zeros((8, NZ), jnp.float32)

    def passes(u0, u1):
        def pass1(e, m0):
            add = acc0
            for i in CHUNKS:
                kk = k[e, part(i)]
                rr = -(kk * stencil(u0, e, i))
                r[e, part(i)] = rr
                u1[e, part(i)] = kk * rr
                add = add + inner(rr * rr, i)
            return m0 + weight(e) * add

        def pass2(e, m):
            add1 = add2 = acc0
            for i in CHUNKS:
                kk = k[e, part(i)]
                rr = r[e, part(i)]
                qq = rr + kk * stencil(u1, e, i)
                q[e, part(i)] = qq
                u0[e, part(i)] = kk * qq
                add1 = add1 + inner(rr * qq, i)
                add2 = add2 + inner(qq * qq, i)
            return m[0] + weight(e) * add1, m[1] + weight(e) * add2

        def pass3(e, m3):
            for i in CHUNKS:
                m3 = m3 + inner(u0[e, part(i)] * stencil(u0, e, i), i)
            return m3

        return pass1, pass2, pass3

    def scalars(ms, g, beside=None):
        rows = []
        for m in ms:
            v = jnp.sum(m, axis=0, keepdims=True)
            w = v[:, :LANES]
            for i in range(1, NZ // LANES):
                w = w + v[:, i * LANES:(i + 1) * LANES]
            rows.append(w)
        rows.append(jnp.zeros((4, LANES), jnp.float32))
        red[g, s] = jnp.concatenate(rows, axis=0)
        sends, recvs = peer_copies(lambda j: red.at[g, j], a_send.at[g], a_recv.at[g])
        for c in sends:
            c.start()
        if beside is not None:
            beside()
        for c in recvs:
            c.wait_recv()
        tot = red[g, 0]
        for j in range(1, S):
            tot = tot + red[g, j]
        tot = jnp.sum(tot, axis=1, keepdims=True)
        m0, m1, m2, m3 = (tot[i:i + 1] for i in range(4))
        a0 = m0 / m1
        rr1 = m0 - 2.0 * a0 * m1 + a0 * a0 * m2
        g1 = 1.0 + rr1 / m0
        curv = g1 * g1 * m1 - 2.0 * g1 * a0 * m2 + a0 * a0 * m3
        a1 = rr1 / curv
        return a0 + a1 * g1, -(a1 * a0), sends

    def first(e, _):
        ua[e] = k[e] * b[e]
        return 0

    pass1, pass2, pass3 = passes(ua, ub)
    lax.fori_loop(W, W + PL, first, 0)
    m0 = lax.fori_loop(W + 1, W + PL - 1, pass1, acc0)
    m12 = lax.fori_loop(W + 2, W + PL - 2, pass2, (acc0, acc0))

    halo = [(e, has_dn, (e + PL - W) % 2) for e in range(W)]
    halo += [(e, has_up, (e - PL - W) % 2) for e in range(W + PL, E)]
    for e, has, _ in halo:
        @pl.when(has)
        def _(e=e):
            plane_recv(b, e, b_ysend.at[0], b_recv).wait_recv()
    for e, has, parity in halo:
        @pl.when(has & (par == parity))
        def _(e=e):
            plane_recv(k, e, k_ysend.at[0], k_recv).wait_recv()
            sib_copy(e).start()
    for e, has, parity in halo:
        @pl.when(has & (par != parity))
        def _(e=e):
            plane_recv(k, e, k_ysend.at[0], k_recv).wait_recv()

    lax.fori_loop(0, W, first, 0)
    lax.fori_loop(W + PL, E, first, 0)
    m0 = lax.fori_loop(1, W + 1, pass1, m0)
    m0 = lax.fori_loop(W + PL - 1, E - 1, pass1, m0)
    m12 = lax.fori_loop(2, W + 2, pass2, m12)
    m12 = lax.fori_loop(W + PL - 2, E - 2, pass2, m12)
    m3 = lax.fori_loop(W, W + PL, pass3, m12[1])
    c1, c2, sends1 = scalars((m0,) + m12 + (m3,), 0)

    def update(e, _):
        x = b[e] + c1 * r[e] + c2 * q[e]
        b[e] = x
        ua[e] = k[e] * x
        return 0

    for t in range(L):
        y_copy(st_ref.at[0], b, t, b_ysend, b_recv).wait_send()
    for pp in range(PL):
        z_each(b, pp, b_zsend, b_recv, always, wait_send)
    lax.fori_loop(2, E - 2, update, 0)
    def coarse_of(first):
        return jnp.concatenate([gath[j, first:first + LC] for j in range(S)], axis=0)

    def moved(a):
        return (
            jnp.concatenate([a[:1], a[:-1]], axis=0),
            jnp.concatenate([a[1:], a[-1:]], axis=0),
            pltpu.roll(a, 1, 1),
            pltpu.roll(a, YC - 1, 1),
            pltpu.roll(a, 1, 2),
            pltpu.roll(a, LANES - 1, 2),
        )

    def coarse_setup():
        for c in gr:
            c.wait_recv()

        K = coarse_of(LC)
        shape = (XC, YC, LANES)
        row = lax.broadcasted_iota(jnp.int32, shape, 1)
        lane = lax.broadcasted_iota(jnp.int32, shape, 2)
        pad = lane >= ZC

        plane = lax.broadcasted_iota(jnp.int32, shape, 0)
        edges = (plane == 0, plane == XC - 1, row == 0, row == YC - 1, lane == 0, lane == ZC - 1)
        diag = jnp.ones(shape, jnp.float32)
        for i, (near, edge) in enumerate(zip(moved(K), edges)):
            coef = 0.15 * (K + jnp.where(edge, K, near))
            diag = diag + coef
            coefs[i] = jnp.where(edge | pad, 0.0, coef)
        rdiag[...] = 1.0 / diag

    m0 = lax.fori_loop(3, E - 3, pass1, acc0)
    m12 = lax.fori_loop(4, E - 4, pass2, (acc0, acc0))
    m3 = lax.fori_loop(W, W + PL, pass3, m12[1])
    c1, c2, sends2 = scalars((m0,) + m12 + (m3,), 1, coarse_setup)

    rows_in = slice(RH, RH + HY)
    for pc in range(PL // FACTOR):
        def last(j, acc, pc=pc):
            i = pc * FACTOR + j
            e = W + i
            x = b[e, rows_in, :] + c1 * r[e, rows_in, :] + c2 * q[e, rows_in, :]
            xf[i] = x
            return acc + x

        xsum = lax.fori_loop(0, FACTOR, last, jnp.zeros((HY, NZ), jnp.float32))
        ey = quarter((HY // FACTOR, HY), 1)
        ce[s, pc] = mm(mm(ey, xsum), S_EZ) * scale

    cs, cr = peer_copies(lambda j: ce.at[j], c_send, c_recv)
    for c in cs:
        c.start()

    def end_copy(same):
        half = h if same else 1 - h
        to = s if same else partner
        i = 0 if same else 1
        rows = pl.ds(pl.multiple_of(h * HY, 8), HY)
        return remote(
            xf.at[pl.ds(half * L, L)], fe.at[:, rows, :], e_send.at[i], e_recv.at[i], dev(tm + 1, to)
        )

    def end_recv(same):
        src_half = h if same else 1 - h
        i = 0 if same else 1
        ref = fe.at[:, pl.ds(pl.multiple_of(src_half * HY, 8), HY), :]
        return remote(ref, ref, e_send.at[i], e_recv.at[i], dev(tm - 1, s))

    has_next = tm < T - 1

    @pl.when(has_next)
    def _():
        end_copy(False).start()

    for c in cr:
        c.wait_recv()

    HC = HY // FACTOR
    for j in range(S):
        path_ref[0, (j // 2) * 2 * LC:(j // 2 + 1) * 2 * LC, (j % 2) * HC:(j % 2 + 1) * HC, :] = ce[j, :, :, :ZC]

    def relay_path():
        return remote(pout, pin, p_send.at[0], p_recv.at[0], dev(tm + 1, s))

    pout = coefs.at[6]

    def relay_d():
        return remote(dsend, din, p_send.at[1], p_recv.at[1], dev(tm + 1, s))

    def ce_full():
        blocks = []
        for j in range(0, S, 2):
            blocks.append(jnp.concatenate([ce[j], ce[j + 1]], axis=1))
        return jnp.concatenate(blocks, axis=0)

    @pl.when(tm == 0)
    def _():
        pout[...] = ce_full()
        dsend[...] = jnp.zeros((LC, YC, LANES), jnp.float32)

    @pl.when(tm > 0)
    def _():
        remote(pin, pin, p_send.at[0], p_recv.at[0], dev(tm - 1, s)).wait_recv()
        remote(din, din, p_send.at[1], p_recv.at[1], dev(tm - 1, s)).wait_recv()
        src = pin[...] - coarse_of(0)
        w = src
        for _i in range(JACOBI):
            acc = src
            for i, near in enumerate(moved(w)):
                acc = acc + coefs[i] * near
            w = acc * rdiag[...]
        pout[...] = w
        dsend[...] = coefs[6, pl.ds(s * LC, LC)]
        pth = w + ce_full()
        pout[...] = pth
        path_ref[0] = pth[:, :, :ZC]

    @pl.when(has_next)
    def _():
        relay_path().start()
        relay_d().start()
        end_copy(True).start()

    @pl.when(tm == 0)
    def _():
        out_ref[...] = st_ref[...]

    @pl.when(tm > 0)
    def _():
        end_recv(True).wait_recv()
        end_recv(False).wait_recv()
        for lc in range(LC):
            up = mm(mm(S_EY, din[lc]), S_EZT)
            for j in range(FACTOR):
                i = lc * FACTOR + j
                out_ref[0, i] = fe[i] + up

    for t in range(L):
        @pl.when(par == t % 2)
        def _(t=t):
            y_copy(k_slab, k, t, k_ysend, k_recv).wait_send()
            sib_copy(W + (1 - h) * L + t).wait_send()
    for pp in range(PL):
        z_each(k, pp, k_zsend, k_recv, par == pp % 2, wait_send)
    for e, has, parity in halo:
        @pl.when(has & (par == parity))
        def _(e=e):
            sib_copy(e).wait_send()
    for c in gs + sends1 + sends2 + cs:
        c.wait_send()

    @pl.when(has_next)
    def _():
        end_copy(False).wait_send()
        end_copy(True).wait_send()
        relay_path().wait_send()
        relay_d().wait_send()


def local(T, S, starts, material, conductivity):
    _, L, NY, NZ = starts.shape
    E = 2 * L + 2 * W
    HY = NY // 2
    RE = HY + 2 * RH
    LC = L // FACTOR
    XC, YC, ZC = LC * S, NY // FACTOR, NZ // FACTOR
    f32 = jnp.float32
    ext = pltpu.VMEM((E, RE, NZ), f32)
    dma = pltpu.SemaphoreType.DMA
    vm = pl.BlockSpec(memory_space=pltpu.VMEM)
    return pl.pallas_call(
        functools.partial(kernel, T, S, L, NY, NZ, conductivity.shape[0]),
        out_shape=(
            jax.ShapeDtypeStruct(starts.shape, f32),
            jax.ShapeDtypeStruct((1, XC, YC, ZC), f32),
        ),
        in_specs=[pl.BlockSpec(memory_space=pltpu.SMEM), vm, vm],
        out_specs=(vm, vm),
        scratch_shapes=[
            pltpu.VMEM((L, NY, NZ), f32), ext, ext, ext, ext, ext, ext,
            pltpu.VMEM((2 * L, HY, NZ), f32), pltpu.VMEM((L, NY, NZ), f32),
            pltpu.VMEM((2, S, 8, LANES), f32),
            pltpu.VMEM((S, 2 * LC, YC, LANES), f32),
            pltpu.VMEM((S, 2 * LC, YC // 2, LANES), f32),
            pltpu.VMEM((XC, YC, LANES), f32),
            pltpu.VMEM((LC, YC, LANES), f32),
            pltpu.VMEM((LC, YC, LANES), f32),
            pltpu.VMEM((7, XC, YC, LANES), f32),
            pltpu.VMEM((XC, YC, LANES), f32),
            dma((E,)), dma((E,)), dma((L,)), dma((L,)), dma((2, 2 * L)), dma((2, 2 * L)), dma((E,)),
            dma((2, S)), dma((2, S)), dma((S,)), dma((S,)), dma((S,)), dma((S,)),
            dma((2,)), dma((2,)), dma((2,)), dma((2,)),
        ],
        compiler_params=pltpu.CompilerParams(
            collective_id=0, has_side_effects=True, vmem_limit_bytes=60 * 1024 * 1024
        ),
    )(conductivity, starts, material)


def solution(mesh):
    return jax.shard_map(
        functools.partial(local, mesh.shape["tm"], mesh.shape["space"]),
        mesh=mesh,
        in_specs=(P("tm", "space", None, None), P("space", None, None), P()),
        out_specs=(P("tm", "space", None, None), P("tm", None, None, None)),
        check_vma=False,
    )
```
